32 devices in a mesh: ue: 8 (over z, y), cell: 4 (over x, core).
Axes of the slice: x: 2, y: 2, z: 4, core: 2. Of those that a mesh axis runs over, the one named last changes fastest.
Arguments:
- gains: bfloat16 [512, 16, 128, 128], P('ue', 'cell'), may hold values from 0 to 4.8828125
- near_blocks: int32 [512, 16], P('ue', 'cell'), may hold values from 0 to 31, as said below
- serve_block: int32 [65536, 1], P(('ue', 'cell')), may hold values from 0 to 31; in each aligned block of 2048 rows (0 to 2047, 2048 to 4095, ...) at most 192 rows name the same one
- serve_cell: int32 [65536], P(('ue', 'cell')), may hold values from 0 to 127
- serve_gain: float32 [65536], P(('ue', 'cell')), may hold values from 0.2 to 5
- power_init: float32 [32, 4096], P(None, ('ue', 'cell')), may hold values from 0.01 to 2
- avg_init: float32 [65536], P(('ue', 'cell')), may hold values from 0.05 to 1
Outputs:
- avg_out: float32 [65536], P(('ue', 'cell'))
- power_out: float32 [32, 4096], P(None, ('ue', 'cell'))
The draws below stay inside these ranges and needn't reach their ends.
Inputs may be any that keep to these rules, and one draw needn't show every extreme that they name: `near_blocks`: for each UE block, the entries in columns j * 4 to (j + 1) * 4 - 1 are distinct cell blocks, each equal to j modulo 4. `serve_block`: within the 2048 UEs of each aligned block, at most 192 have the same serving cell block, and some cell block serves exactly 192 of them.
All inputs are finite; a program needn't handle non-finite values.
Results may differ from the reference program's by a relative error of at most 0.002.
Values may be sent and summed in bfloat16 or wider, within the bound.
A program may use at most 128 MiB of HBM per device.

```python
import math
import jax
import jax.numpy as jnp
import numpy as np
from jax import lax

SUBBANDS = 32
BLK = 128
UE_DEV = 2048
NEAR_DEV = 4
SLOTS = 4
GROUPS = 4
UE_GROUPS = 8
CAP = 192
UES = 65536
CELL_BLOCKS = 32
CELLS = 4096
UE_BLOCKS = 512


def near_table(key):
    scores = jax.random.randint(key, (UE_BLOCKS, GROUPS, UE_GROUPS), 0, 1 << 20)
    scores = scores * UE_GROUPS + jnp.arange(UE_GROUPS, dtype=jnp.int32)[None, None, :]
    order = jnp.argsort(scores, axis=-1)
    picked = order[:, :, :NEAR_DEV].astype(jnp.int32)
    blocks = jnp.arange(GROUPS, dtype=jnp.int32)[None, :, None] + GROUPS * picked
    return blocks.reshape(UE_BLOCKS, GROUPS * NEAR_DEV).astype(jnp.int32)


def cell_log_factor(key):
    return jax.random.uniform(jax.random.fold_in(key, 31), (CELLS,), jnp.float32, -2.5, 2.5)


def draw_near_blocks(key, part):
    return near_table(key)


def draw_gains(key, part):
    shape = (UE_BLOCKS, NEAR_DEV * GROUPS, BLK, BLK)
    terms_total = NEAR_DEV * GROUPS * BLK
    near = near_table(key)
    log_factor = cell_log_factor(key).reshape(CELL_BLOCKS, BLK)
    factor = jnp.exp(log_factor[near])[:, :, :, None]
    level = jnp.clip(jax.random.normal(jax.random.fold_in(key, 11), shape, jnp.float32), -4.0, 4.0)
    values = 4.0 / terms_total * factor * jnp.exp(1.2 * level) / 5.0
    return values.astype(jnp.float32).astype(jnp.bfloat16)


def draw_power_init(key, part):
    log_factor = cell_log_factor(key)[None, :]
    noise = jax.random.uniform(jax.random.fold_in(key, 41), (SUBBANDS, CELLS), jnp.float32, 0.0, 1.0)
    mixed = 0.7 * (2.5 - log_factor) / 5.0 + 0.3 * noise
    mixed = jnp.clip(mixed, 0.0, 1.0)
    return (0.01 * jnp.exp(5.298317 * mixed)).astype(jnp.float32)


def place_ends(result, own_key, smallest, largest):
    longest = result.shape.index(max(result.shape))
    spots = []
    for shift in (0, 1):
        where = [jax.random.randint(jax.random.fold_in(own_key, axis), (), 0, length) for axis, length in enumerate(result.shape)]
        where[longest] = (where[longest] + shift) % result.shape[longest]
        spots.append(tuple(where))
    return result.at[spots[0]].set(smallest).at[spots[1]].set(largest)


def block_scale(rng, extent, split, least, largest):
    def one(dim, parts):
        draws = jax.random.uniform(jax.random.fold_in(jax.random.fold_in(rng, 6), dim), (parts,), jnp.float32, least / len(split), largest / len(split))
        return jnp.repeat(jnp.exp(draws), extent[dim] // parts).reshape((-1,) + (1,) * (len(extent) - dim - 1))

    gain = one(*split[0])
    for cut in split[1:]:
        gain = gain * one(*cut)
    return gain


def routed_block(stream_key, own, number, rows, count, top, reach, slope):
    ranking = jax.random.permutation(stream_key, count)
    crowded, common = portions_of(count, rows * top, reach, slope, True), portions_of(count, rows * top, reach, slope, False)
    places = jnp.arange(count)

    def named(lengths, rotation):
        used = int((lengths > 0).sum())
        fixed = max(1, used // 4)
        moved = fixed + (places - fixed + rotation * (used - fixed)) % max(1, count - fixed)
        return jnp.zeros((count,), jnp.int32).at[ranking[jnp.where(places < fixed, places, moved)]].set(jnp.asarray(lengths, jnp.int32))

    lengths = jnp.where(number % 4 == 0, named(crowded, number // 4), named(common, number - number // 4 - 1))
    mixed = jax.random.permutation(jax.random.fold_in(own, 3), count)
    giver, sink = mixed[0:count // 2 * 2:2], mixed[1:count // 2 * 2:2]
    room = jnp.minimum(lengths[giver] - 1, reach - lengths[sink]) // 2
    room = jnp.where((giver == ranking[0]) | (sink == ranking[0]) | (lengths[sink] == 0), 0, jnp.maximum(room, 0))
    moved = jax.random.randint(jax.random.fold_in(own, 4), (count // 2,), 0, 1 << 20) % (room + 1)
    lengths = lengths.at[giver].add(-moved).at[sink].add(moved)
    members = jnp.searchsorted(jnp.cumsum(lengths), jnp.arange(rows * top), side="right").astype(jnp.int32)
    listing = members.reshape(top, rows).T
    listing = listing[jax.random.permutation(jax.random.fold_in(own, 1), rows)]
    rotation = jax.random.randint(jax.random.fold_in(own, 2), (rows, 1), 0, top)
    return jnp.take_along_axis(listing, (jnp.arange(top)[None, :] + rotation) % top, axis=1)


def portions_of(number_of, total, most, lean, full):
    loads = [(1 << 20) // math.isqrt(grade ** lean) + 1 for grade in range(1, number_of + 1)]
    largest = most if full else min(most, max(-(-total // number_of), total * loads[0] // sum(loads)))
    least = 1 if total - largest >= number_of - 1 else 0
    given, surplus = [largest] + [least] * (number_of - 1), total - largest - least * (number_of - 1)
    while surplus > 0:
        candidates = [i for i in range(1, number_of) if given[i] < largest] or [i for i in range(1, number_of) if given[i] < most]
        whole, remaining = sum([loads[i] for i in candidates]), surplus
        for i in candidates:
            more = min(most - given[i], max(1, remaining * loads[i] // whole), surplus)
            given[i] = given[i] + more
            surplus = surplus - more
    return np.array(given)


def setup_inputs(seed: int = 0) -> dict:
    splits = jax.random.split(jax.random.key(seed), 8)
    gains = draw_gains(jax.random.fold_in(splits[7], 71), 0)
    near_blocks = draw_near_blocks(jax.random.fold_in(splits[7], 71), 0)
    serve_block_keys = jax.random.split(jax.random.fold_in(splits[2], 1), UES // UE_DEV)
    serve_block_turns = jax.random.permutation(jax.random.fold_in(splits[2], 3), UES // UE_DEV)
    serve_block = jax.vmap(lambda own, number: routed_block(jax.random.fold_in(splits[2], 2), own, number, UE_DEV, CELL_BLOCKS, 1, CAP, 2))(serve_block_keys, serve_block_turns).reshape((UES, 1))
    serve_cell = place_ends(jax.random.randint(splits[3], (UES,), 0, BLK), jax.random.fold_in(splits[3], 1), 0, BLK - 1).astype(jnp.int32)
    serve_gain = jnp.clip(jnp.exp(math.log(5.0) - 3.218876 * jax.random.uniform(splits[4], (UES,), jnp.float32) ** block_scale(splits[4], (UES,), ((0, 32),), -0.2, 0.2)), 0.2, 5.0)
    power_init = draw_power_init(jax.random.fold_in(splits[7], 71), 0)
    avg_init = jnp.clip(jnp.exp(math.log(1.0) - 2.9957323 * jax.random.uniform(splits[6], (UES,), jnp.float32) ** block_scale(splits[6], (UES,), ((0, 32),), -0.2, 0.2)), 0.05, 1.0)
    return {"gains": gains, "near_blocks": near_blocks, "serve_block": serve_block, "serve_cell": serve_cell, "serve_gain": serve_gain, "power_init": power_init, "avg_init": avg_init}


NOISE_FLOOR = 0.5
KEEP_RATE = 0.7
NEW_RATE = 0.3


def block_terms(power_table, gains, near_blocks):
    group_size = 8
    weight_groups = gains.reshape(UE_BLOCKS // group_size, group_size, NEAR_DEV * GROUPS, BLK, BLK)
    index_groups = near_blocks.reshape(UE_BLOCKS // group_size, group_size, NEAR_DEV * GROUPS)

    def one_group(pair):
        weight_piece, index_piece = pair
        chosen = power_table[index_piece]
        return jnp.einsum("bksw,bkwv->bsv", chosen.astype(jnp.float32), weight_piece.astype(jnp.float32))

    summed = lax.map(one_group, (weight_groups, index_groups))
    summed = summed.reshape(UE_BLOCKS, SUBBANDS, BLK)
    return summed.transpose(1, 0, 2).reshape(SUBBANDS, UES)


def reference(gains, near_blocks, serve_block, serve_cell, serve_gain, power_init, avg_init):
    cell_index = (serve_block[:, 0] * BLK + serve_cell).astype(jnp.int32)
    power_state = power_init
    average = avg_init
    for turn_index in range(SLOTS):
        low_power = power_state.astype(jnp.bfloat16)
        power_table = low_power.reshape(SUBBANDS, CELL_BLOCKS, BLK).transpose(1, 0, 2)
        levels = block_terms(power_table, gains, near_blocks)
        signal = serve_gain[None, :] * power_state[:, cell_index]
        log_rate = jnp.log1p(signal / (levels + NOISE_FLOOR))
        metric = log_rate / average[None, :]
        cell_load = jax.ops.segment_sum(metric.T, cell_index, num_segments=CELLS).T
        shares = metric / cell_load[:, cell_index]
        average = KEEP_RATE * average + NEW_RATE * jnp.sum(shares * log_rate, axis=0)
        demand = 1.0 + cell_load
        power_state = 0.5 * power_state + 0.5 * SUBBANDS * demand / jnp.sum(demand, axis=0, keepdims=True)
    return average, power_state
```

```python
import functools

import jax
import jax.numpy as jnp
from jax import lax
from jax.experimental import pallas as pl
from jax.experimental.pallas import tpu as pltpu
from jax.sharding import PartitionSpec as P

SLOTS = 4
NOISE_FLOOR = 0.5
KEEP_RATE = 0.7
NEW_RATE = 0.3
MESH = pl.DeviceIdType.MESH


def planner(
    ue_count, cell_count,
    gains_hbm, near, block_ref, cell_ref, gain_ref, power_ref, avg_ref,
    avg_out, power_out,
    gains, high, low, power, loads, tails, mine, parts_in, parts_out, terms_in, terms_out,
    levels, signal_power, log_rates, metrics, spread, pick_cell, put_cell,
    gains_sem, terms_send, terms_recv, parts_send, parts_recv, loads_send, loads_recv,
    tails_send, tails_recv,
):
    device_count = ue_count * cell_count
    ue_at, cell_at = lax.axis_index("ue"), lax.axis_index("cell")
    me = ue_at * cell_count + cell_at
    home_blocks, subbands, width = levels.shape
    near_count = near.shape[0] // gains.shape[0]
    pairs = home_blocks // 2
    f32, bf16 = jnp.float32, jnp.bfloat16

    def device(number):
        return (number // cell_count, lax.rem(number, cell_count))

    barrier = pltpu.get_barrier_semaphore()

    def greet(step, carry):
        pl.semaphore_signal(
            barrier, inc=1, device_id=device(lax.rem(me + step, device_count)), device_id_type=MESH
        )
        return carry

    lax.fori_loop(1, device_count, greet, 0)

    def gains_copy(chunk):
        rows = pl.ds(chunk * home_blocks, home_blocks)
        return pltpu.make_async_copy(gains_hbm.at[rows], gains.at[rows], gains_sem.at[chunk])

    for step in range(1, cell_count + 1):
        gains_copy(lax.rem(cell_at + step, cell_count)).start()
    pl.semaphore_wait(barrier, device_count - 1)

    def spread_copy(table, send_sem, recv_sem, step):
        return pltpu.make_async_remote_copy(
            src_ref=table.at[me], dst_ref=table.at[me],
            send_sem=send_sem.at[step], recv_sem=recv_sem.at[step],
            device_id=device(lax.rem(me + step, device_count)), device_id_type=MESH,
        )

    def spread_arrival(table, send_sem, recv_sem, step):
        source = lax.rem(me - step + device_count, device_count)
        return pltpu.make_async_remote_copy(
            src_ref=table.at[source], dst_ref=table.at[source],
            send_sem=send_sem.at[step], recv_sem=recv_sem.at[step],
            device_id=device(source), device_id_type=MESH,
        )

    main = (loads, loads_send, loads_recv)
    rest = (tails, tails_send, tails_recv)

    def split_load(value):
        top = value.astype(bf16)
        loads[me] = top
        tails[me] = (value - top.astype(f32)).astype(bf16)

    def whole_load(block):
        return loads[block].astype(f32) + tails[block].astype(f32)

    def parts_copy(owner):
        step = lax.rem(owner - me + device_count, device_count)
        return pltpu.make_async_remote_copy(
            src_ref=parts_out.at[owner], dst_ref=parts_in.at[step],
            send_sem=parts_send.at[step], recv_sem=parts_recv.at[step],
            device_id=device(owner), device_id_type=MESH,
        )

    def terms_copy(step):
        target = lax.rem(cell_at + step, cell_count)
        return pltpu.make_async_remote_copy(
            src_ref=terms_out.at[step], dst_ref=terms_in.at[step],
            send_sem=terms_send.at[step], recv_sem=terms_recv.at[step],
            device_id=(ue_at, target), device_id_type=MESH,
        )

    def each_peer(action):
        def body(step, carry):
            action(step)
            return carry

        lax.fori_loop(1, device_count, body, 0)

    def set_power(block, value):
        power[block] = value
        top = value.astype(bf16)
        high[block] = top
        low[block] = (value - top.astype(f32)).astype(bf16)

    def next_power(value, load):
        demand = 1.0 + load
        scale = (0.5 * subbands) / jnp.sum(demand, axis=0, keepdims=True)
        return 0.5 * value + demand * scale

    mine[...] = power_ref[...]
    split_load(power_ref[...])
    each_peer(lambda step: spread_copy(*main, step).start())
    each_peer(lambda step: spread_copy(*rest, step).start())
    spots = lax.broadcasted_iota(jnp.int32, (width, width), 0)
    for home in range(home_blocks):
        hot = (spots == cell_ref[home]).astype(f32)
        columns = slice((home % 2) * width, (home % 2 + 1) * width)
        pick_cell[home // 2, 0:width, columns] = hot.astype(bf16)
        pick_cell[home // 2, width : 2 * width, columns] = hot.astype(bf16)
        put_cell[home * width : (home + 1) * width, :] = hot.T.astype(bf16)
        avg_out[home] = avg_ref[home]
    each_peer(lambda step: spread_arrival(*main, step).wait_recv())

    def start_high(block, carry):
        high[block] = loads[block]
        return carry

    lax.fori_loop(0, device_count, start_high, 0)
    each_peer(lambda step: spread_copy(*main, step).wait_send())

    def finish_power(turn):
        each_peer(lambda step: spread_arrival(*rest, step).wait_recv())

        @pl.when(turn == 0)
        def _():
            def first(block, carry):
                set_power(block, whole_load(block))
                return carry

            lax.fori_loop(0, device_count, first, 0)

        @pl.when(turn > 0)
        def _():
            def later(block, carry):
                set_power(block, next_power(power[block], whole_load(block)))
                return carry

            lax.fori_loop(0, device_count, later, 0)

        set_power(me, mine[...])
        each_peer(lambda step: spread_copy(*rest, step).wait_send())

    def terms(target, step):
        def body(group, carry):
            for inner in range(4):
                home = group * 4 + inner
                block = target * home_blocks + home
                chosen = jnp.concatenate(
                    [high[near[block * near_count + k]] for k in range(near_count)], axis=1
                )
                total = jnp.dot(chosen, gains[block], preferred_element_type=f32)
                if step == cell_count:
                    levels[home] = total
                else:
                    terms_out[step, home] = total.astype(bf16)
            return carry

        lax.fori_loop(0, home_blocks // 4, body, 0)

    group_blocks = 16

    def gather(table, result):
        def body(pair, carry):
            names = jnp.concatenate([block_ref[2 * pair], block_ref[2 * pair + 1]], axis=1)
            total = jnp.zeros((subbands, 2 * width), f32)
            for first in range(0, device_count, group_blocks):
                left = table(first)
                found = jnp.dot(
                    left, pick_cell[pair, 0 : left.shape[1], :], preferred_element_type=f32
                )
                for inner in range(group_blocks):
                    total = jnp.where(
                        names == first + inner,
                        found[inner * subbands : (inner + 1) * subbands],
                        total,
                    )
            result[2 * pair] = total[:, :width]
            result[2 * pair + 1] = total[:, width:]
            return carry

        lax.fori_loop(0, pairs, body, 0)

    def power_rows(first):
        rows = slice(first, first + group_blocks)
        both = jnp.concatenate([high[rows], low[rows]], axis=2)
        return both.reshape(group_blocks * subbands, 2 * width)

    def load_rows(first):
        return loads[first : first + group_blocks].reshape(group_blocks * subbands, width)

    def finish_average():
        gather(load_rows, spread)
        for home in range(home_blocks):
            share = metrics[home] / spread[home]
            gained = jnp.sum(share * log_rates[home], axis=0, keepdims=True)
            avg_out[home] = KEEP_RATE * avg_out[home] + NEW_RATE * gained

    piece = 8

    def slot(turn, carry):
        for step in range(1, cell_count + 1):
            target = lax.rem(cell_at + step, cell_count)

            @pl.when(turn == 0)
            def _():
                gains_copy(target).wait()

            terms(target, step)
            if step < cell_count:
                terms_copy(step).start()

        @pl.when(turn > 0)
        def _():
            finish_average()

        finish_power(turn)
        gather(power_rows, signal_power)
        for step in range(1, cell_count):
            terms_copy(step).wait_recv()
        for home in range(home_blocks):
            level = levels[home]
            for step in range(1, cell_count):
                level = level + terms_in[step, home].astype(f32)
            signal = gain_ref[home] * signal_power[home]
            rate = jnp.log1p(signal / (level + NOISE_FLOOR))
            log_rates[home] = rate
            metrics[home] = rate / avg_out[home]
        names = jnp.concatenate([block_ref[home] for home in range(home_blocks)], axis=1)

        def scatter(index, inner_carry):
            first = lax.rem(me // piece + 1 + index, device_count // piece) * piece
            metric = jnp.concatenate([metrics[home] for home in range(home_blocks)], axis=1)
            left = jnp.concatenate(
                [
                    jnp.where(names == first + inner, metric, 0.0).astype(bf16)
                    for inner in range(piece)
                ],
                axis=0,
            )
            summed = jnp.dot(left, put_cell[...], preferred_element_type=f32)
            for inner in range(piece):
                owner = first + inner
                parts_out[owner] = summed[inner * subbands : (inner + 1) * subbands].astype(bf16)

                @pl.when(owner != me)
                def _():
                    parts_copy(owner).start()

            return inner_carry

        lax.fori_loop(0, device_count // piece, scatter, 0)
        for step in range(1, cell_count):
            terms_copy(step).wait_send()

        def add(step, total):
            parts_copy(lax.rem(me + step, device_count)).wait_recv()
            return total + parts_in[step].astype(f32)

        load = lax.fori_loop(1, device_count, add, parts_out[me].astype(f32))
        split_load(load)
        each_peer(lambda step: spread_copy(*main, step).start())

        @pl.when(turn < SLOTS - 1)
        def _():
            each_peer(lambda step: spread_copy(*rest, step).start())

        mine[...] = next_power(mine[...], load)
        each_peer(lambda step: parts_copy(lax.rem(me + step, device_count)).wait_send())
        each_peer(lambda step: spread_arrival(*main, step).wait_recv())

        @pl.when(turn < SLOTS - 1)
        def _():
            def update(block, inner_carry):
                high[block] = next_power(power[block], loads[block].astype(f32)).astype(bf16)
                return inner_carry

            lax.fori_loop(0, device_count, update, 0)
            high[me] = mine[...].astype(bf16)

        each_peer(lambda step: spread_copy(*main, step).wait_send())
        return carry

    lax.fori_loop(0, SLOTS, slot, 0)
    finish_average()
    power_out[...] = mine[...]


def on_device(gains, near_blocks, serve_block, serve_cell, serve_gain, power_init, avg_init):
    ue_count = lax.axis_size("ue")
    cell_count = lax.axis_size("cell")
    device_count = ue_count * cell_count
    blocks, near_count, width, _ = gains.shape
    rows = serve_gain.shape[0]
    homes = rows // width
    subbands = power_init.shape[0]
    f32, bf16 = jnp.float32, jnp.bfloat16
    in_vmem = pl.BlockSpec(memory_space=pltpu.VMEM)
    table = (device_count, subbands, width)
    home = (homes, subbands, width)
    row = (homes, 1, width)
    average, power = pl.pallas_call(
        functools.partial(planner, ue_count, cell_count),
        out_shape=(
            jax.ShapeDtypeStruct(row, f32),
            jax.ShapeDtypeStruct(power_init.shape, f32),
        ),
        in_specs=[
            pl.BlockSpec(memory_space=pl.ANY),
            pl.BlockSpec(memory_space=pltpu.SMEM),
        ]
        + [in_vmem] * 5,
        out_specs=(in_vmem, in_vmem),
        scratch_shapes=[
            pltpu.VMEM((blocks, near_count * width, width), bf16),
            pltpu.VMEM(table, bf16),
            pltpu.VMEM(table, bf16),
            pltpu.VMEM(table, f32),
            pltpu.VMEM(table, bf16),
            pltpu.VMEM(table, bf16),
            pltpu.VMEM((subbands, width), f32),
            pltpu.VMEM(table, bf16),
            pltpu.VMEM(table, bf16),
            pltpu.VMEM((cell_count,) + home, bf16),
            pltpu.VMEM((cell_count,) + home, bf16),
            pltpu.VMEM(home, f32),
            pltpu.VMEM(home, f32),
            pltpu.VMEM(home, f32),
            pltpu.VMEM(home, f32),
            pltpu.VMEM(home, f32),
            pltpu.VMEM((homes // 2, 2 * width, 2 * width), bf16),
            pltpu.VMEM((rows, width), bf16),
            pltpu.SemaphoreType.DMA((cell_count,)),
            pltpu.SemaphoreType.DMA((cell_count,)),
            pltpu.SemaphoreType.DMA((cell_count,)),
            pltpu.SemaphoreType.DMA((device_count,)),
            pltpu.SemaphoreType.DMA((device_count,)),
            pltpu.SemaphoreType.DMA((device_count,)),
            pltpu.SemaphoreType.DMA((device_count,)),
            pltpu.SemaphoreType.DMA((device_count,)),
            pltpu.SemaphoreType.DMA((device_count,)),
        ],
        compiler_params=pltpu.CompilerParams(
            collective_id=0, has_side_effects=True, vmem_limit_bytes=48 * 1024 * 1024
        ),
    )(
        gains.reshape(blocks, near_count * width, width),
        near_blocks.reshape(-1),
        serve_block.reshape(row),
        serve_cell.reshape(row),
        serve_gain.reshape(row),
        power_init,
        avg_init.reshape(row),
    )
    return (average.reshape(rows), power)


def solution(mesh):
    return jax.shard_map(
        on_device,
        mesh=mesh,
        in_specs=(
            P("ue", "cell", None, None),
            P("ue", "cell"),
            P(("ue", "cell"), None),
            P(("ue", "cell")),
            P(("ue", "cell")),
            P(None, ("ue", "cell")),
            P(("ue", "cell")),
        ),
        out_specs=(P(("ue", "cell")), P(None, ("ue", "cell"))),
        check_vma=False,
    )
```

```python
import functools

import jax
import jax.numpy as jnp
from jax import lax
from jax.experimental import pallas as pl
from jax.experimental.pallas import tpu as pltpu
from jax.sharding import PartitionSpec as P

SLOTS = 4
NOISE_FLOOR = 0.5
KEEP_RATE = 0.7
NEW_RATE = 0.3
MESH = pl.DeviceIdType.MESH


def planner(
    ue_count, cell_count,
    gains_hbm, near, block_hbm, cell_hbm, gain_hbm, power_hbm, avg_hbm,
    avg_out, power_out,
    block_ref, cell_ref, gain_ref, gains, high, low, power, loads, tails, mine, parts_in, parts_out, terms_in, terms_out,
    levels, signal_power, log_rates, metrics, spread, pick_cell, put_cell,
    gains_sem, terms_send, terms_recv, parts_send, parts_recv, loads_send, loads_recv,
    tails_send, tails_recv, inputs_sem,
):
    device_count = ue_count * cell_count
    ue_at, cell_at = lax.axis_index("ue"), lax.axis_index("cell")
    me = ue_at * cell_count + cell_at
    home_blocks, subbands, width = levels.shape
    near_count = near.shape[0] // gains.shape[0]
    pairs = home_blocks // 2
    f32, bf16 = jnp.float32, jnp.bfloat16

    def device(number):
        return (number // cell_count, lax.rem(number, cell_count))

    inputs = [
        pltpu.make_async_copy(source, target, inputs_sem.at[place])
        for place, (source, target) in enumerate(
            [
                (power_hbm, mine), (cell_hbm, cell_ref), (block_hbm, block_ref),
                (gain_hbm, gain_ref), (avg_hbm, avg_out),
            ]
        )
    ]
    for copy in inputs:
        copy.start()
    barrier = pltpu.get_barrier_semaphore()

    def greet(step, carry):
        pl.semaphore_signal(
            barrier, inc=1, device_id=device(lax.rem(me + step, device_count)), device_id_type=MESH
        )
        return carry

    lax.fori_loop(1, device_count, greet, 0)

    def gains_copy(chunk):
        rows = pl.ds(chunk * home_blocks, home_blocks)
        return pltpu.make_async_copy(gains_hbm.at[rows], gains.at[rows], gains_sem.at[chunk])

    def terms_target(step):
        chips = cell_count // 2
        chip = lax.rem(cell_at // 2 + step // 2, chips)
        return chip * 2 + lax.rem(cell_at + step, 2)

    terms_order = list(range(2, cell_count)) + [1, 0]
    for step in terms_order:
        gains_copy(terms_target(step)).start()
    for copy in inputs:
        copy.wait()
    pl.semaphore_wait(barrier, device_count - 1)

    def spread_copy(table, send_sem, recv_sem, step):
        return pltpu.make_async_remote_copy(
            src_ref=table.at[me], dst_ref=table.at[me],
            send_sem=send_sem.at[step], recv_sem=recv_sem.at[step],
            device_id=device(lax.rem(me + step, device_count)), device_id_type=MESH,
        )

    def spread_arrival(table, send_sem, recv_sem, step):
        source = lax.rem(me - step + device_count, device_count)
        return pltpu.make_async_remote_copy(
            src_ref=table.at[source], dst_ref=table.at[source],
            send_sem=send_sem.at[step], recv_sem=recv_sem.at[step],
            device_id=device(source), device_id_type=MESH,
        )

    main = (loads, loads_send, loads_recv)
    rest = (tails, tails_send, tails_recv)

    def split_load(value):
        top = value.astype(bf16)
        loads[me] = top
        tails[me] = (value - top.astype(f32)).astype(bf16)

    def whole_load(block):
        return loads[block].astype(f32) + tails[block].astype(f32)

    def parts_copy(owner):
        step = lax.rem(owner - me + device_count, device_count)
        return pltpu.make_async_remote_copy(
            src_ref=parts_out.at[owner], dst_ref=parts_in.at[step],
            send_sem=parts_send.at[step], recv_sem=parts_recv.at[step],
            device_id=device(owner), device_id_type=MESH,
        )

    def terms_copy(step):
        target = terms_target(step)
        return pltpu.make_async_remote_copy(
            src_ref=terms_out.at[step], dst_ref=terms_in.at[step],
            send_sem=terms_send.at[step], recv_sem=terms_recv.at[step],
            device_id=(ue_at, target), device_id_type=MESH,
        )

    def each_peer(action):
        def body(step, carry):
            action(step)
            return carry

        lax.fori_loop(1, device_count, body, 0)

    def each_near(action):
        def body(step, carry):
            action(step * cell_count)
            return carry

        lax.fori_loop(1, ue_count, body, 0)

    def each_far(action):
        def body(step, carry):
            for other in range(1, cell_count):
                action(step * cell_count + other)
            return carry

        lax.fori_loop(0, ue_count, body, 0)

    def set_power(block, value):
        power[block] = value
        top = value.astype(bf16)
        high[block] = top
        low[block] = (value - top.astype(f32)).astype(bf16)

    def next_power(value, load):
        demand = 1.0 + load
        scale = (0.5 * subbands) / jnp.sum(demand, axis=0, keepdims=True)
        return 0.5 * value + demand * scale

    split_load(mine[...])
    each_near(lambda step: spread_copy(*main, step).start())
    each_far(lambda step: spread_copy(*main, step).start())
    each_peer(lambda step: spread_copy(*rest, step).start())
    spots = lax.broadcasted_iota(jnp.int32, (width, width), 0)
    for home in range(home_blocks):
        hot = (spots == cell_ref[home]).astype(f32)
        columns = slice((home % 2) * width, (home % 2 + 1) * width)
        pick_cell[home // 2, 0:width, columns] = hot.astype(bf16)
        pick_cell[home // 2, width : 2 * width, columns] = hot.astype(bf16)
        put_cell[home * width : (home + 1) * width, :] = hot.T.astype(bf16)
    each_near(lambda step: spread_arrival(*main, step).wait_recv())

    def start_high(index, carry):
        block = index * cell_count + cell_at
        high[block] = loads[block]
        return carry

    lax.fori_loop(0, ue_count, start_high, 0)

    def finish_loads():
        each_far(lambda step: spread_arrival(*main, step).wait_recv())
        each_peer(lambda step: spread_copy(*main, step).wait_send())

    def finish_power(turn):
        each_peer(lambda step: spread_arrival(*rest, step).wait_recv())

        @pl.when(turn == 0)
        def _():
            def first(block, carry):
                set_power(block, whole_load(block))
                return carry

            lax.fori_loop(0, device_count, first, 0)

        @pl.when(turn > 0)
        def _():
            def later(block, carry):
                set_power(block, next_power(power[block], whole_load(block)))
                return carry

            lax.fori_loop(0, device_count, later, 0)

        set_power(me, mine[...])
        each_peer(lambda step: spread_copy(*rest, step).wait_send())

    def terms(target, step):
        def body(group, carry):
            for inner in range(4):
                home = group * 4 + inner
                block = target * home_blocks + home
                chosen = jnp.concatenate(
                    [high[near[block * near_count + k]] for k in range(near_count)], axis=1
                )
                total = jnp.dot(chosen, gains[block], preferred_element_type=f32)
                if step == 0:
                    levels[home] = total
                else:
                    terms_out[step, home] = total.astype(bf16)
            return carry

        lax.fori_loop(0, home_blocks // 4, body, 0)

    group_blocks = 16

    def gather(table, result):
        def body(pair, carry):
            names = jnp.concatenate([block_ref[2 * pair], block_ref[2 * pair + 1]], axis=1)
            total = jnp.zeros((subbands, 2 * width), f32)
            for first in range(0, device_count, group_blocks):
                left = table(first)
                found = jnp.dot(
                    left, pick_cell[pair, 0 : left.shape[1], :], preferred_element_type=f32
                )
                for inner in range(group_blocks):
                    total = jnp.where(
                        names == first + inner,
                        found[inner * subbands : (inner + 1) * subbands],
                        total,
                    )
            result[2 * pair] = total[:, :width]
            result[2 * pair + 1] = total[:, width:]
            return carry

        lax.fori_loop(0, pairs, body, 0)

    def power_rows(first):
        rows = slice(first, first + group_blocks)
        both = jnp.concatenate([high[rows], low[rows]], axis=2)
        return both.reshape(group_blocks * subbands, 2 * width)

    def load_rows(first):
        return loads[first : first + group_blocks].reshape(group_blocks * subbands, width)

    def finish_average():
        gather(load_rows, spread)
        for home in range(home_blocks):
            share = metrics[home] / spread[home]
            gained = jnp.sum(share * log_rates[home], axis=0, keepdims=True)
            avg_out[home] = KEEP_RATE * avg_out[home] + NEW_RATE * gained

    piece = 8

    def slot(turn, carry):
        for step in terms_order:
            target = terms_target(step)

            @pl.when(turn == 0)
            def _():
                gains_copy(target).wait()

            terms(target, step)
            if step > 0:
                terms_copy(step).start()

        finish_loads()

        @pl.when(turn > 0)
        def _():
            finish_average()

        finish_power(turn)
        gather(power_rows, signal_power)
        for step in range(1, cell_count):
            terms_copy(step).wait_recv()
        for home in range(home_blocks):
            level = levels[home]
            for step in range(1, cell_count):
                level = level + terms_in[step, home].astype(f32)
            signal = gain_ref[home] * signal_power[home]
            rate = jnp.log1p(signal / (level + NOISE_FLOOR))
            log_rates[home] = rate
            metrics[home] = rate / avg_out[home]
        names = jnp.concatenate([block_ref[home] for home in range(home_blocks)], axis=1)

        def scatter(index, inner_carry):
            first = lax.rem(me // piece + 1 + index, device_count // piece) * piece
            metric = jnp.concatenate([metrics[home] for home in range(home_blocks)], axis=1)
            left = jnp.concatenate(
                [
                    jnp.where(names == first + inner, metric, 0.0).astype(bf16)
                    for inner in range(piece)
                ],
                axis=0,
            )
            summed = jnp.dot(left, put_cell[...], preferred_element_type=f32)
            for inner in range(piece):
                owner = first + inner
                parts_out[owner] = summed[inner * subbands : (inner + 1) * subbands].astype(bf16)

                @pl.when(owner != me)
                def _():
                    parts_copy(owner).start()

            return inner_carry

        lax.fori_loop(0, device_count // piece, scatter, 0)
        for step in range(1, cell_count):
            terms_copy(step).wait_send()

        def add(step, total):
            parts_copy(lax.rem(me + step, device_count)).wait_recv()
            return total + parts_in[step].astype(f32)

        load = lax.fori_loop(1, device_count, add, parts_out[me].astype(f32))
        split_load(load)
        each_near(lambda step: spread_copy(*main, step).start())
        each_far(lambda step: spread_copy(*main, step).start())

        @pl.when(turn < SLOTS - 1)
        def _():
            each_peer(lambda step: spread_copy(*rest, step).start())

        mine[...] = next_power(mine[...], load)
        each_near(lambda step: spread_arrival(*main, step).wait_recv())

        @pl.when(turn < SLOTS - 1)
        def _():
            def update(index, inner_carry):
                block = index * cell_count + cell_at
                high[block] = next_power(power[block], loads[block].astype(f32)).astype(bf16)
                return inner_carry

            lax.fori_loop(0, ue_count, update, 0)
            high[me] = mine[...].astype(bf16)

        each_peer(lambda step: parts_copy(lax.rem(me + step, device_count)).wait_send())
        return carry

    lax.fori_loop(0, SLOTS, slot, 0)
    finish_loads()
    finish_average()
    power_out[...] = mine[...]


def on_device(gains, near_blocks, serve_block, serve_cell, serve_gain, power_init, avg_init):
    ue_count = lax.axis_size("ue")
    cell_count = lax.axis_size("cell")
    device_count = ue_count * cell_count
    blocks, near_count, width, _ = gains.shape
    rows = serve_gain.shape[0]
    homes = rows // width
    subbands = power_init.shape[0]
    f32, bf16 = jnp.float32, jnp.bfloat16
    in_vmem = pl.BlockSpec(memory_space=pltpu.VMEM)
    table = (device_count, subbands, width)
    home = (homes, subbands, width)
    row = (homes, 1, width)
    average, power = pl.pallas_call(
        functools.partial(planner, ue_count, cell_count),
        out_shape=(
            jax.ShapeDtypeStruct(row, f32),
            jax.ShapeDtypeStruct(power_init.shape, f32),
        ),
        in_specs=[
            pl.BlockSpec(memory_space=pl.ANY),
            pl.BlockSpec(memory_space=pltpu.SMEM),
        ]
        + [pl.BlockSpec(memory_space=pl.ANY)] * 5,
        out_specs=(in_vmem, in_vmem),
        scratch_shapes=[
            pltpu.VMEM(row, jnp.int32),
            pltpu.VMEM(row, jnp.int32),
            pltpu.VMEM(row, f32),
            pltpu.VMEM((blocks, near_count * width, width), bf16),
            pltpu.VMEM(table, bf16),
            pltpu.VMEM(table, bf16),
            pltpu.VMEM(table, f32),
            pltpu.VMEM(table, bf16),
            pltpu.VMEM(table, bf16),
            pltpu.VMEM((subbands, width), f32),
            pltpu.VMEM(table, bf16),
            pltpu.VMEM(table, bf16),
            pltpu.VMEM((cell_count,) + home, bf16),
            pltpu.VMEM((cell_count,) + home, bf16),
            pltpu.VMEM(home, f32),
            pltpu.VMEM(home, f32),
            pltpu.VMEM(home, f32),
            pltpu.VMEM(home, f32),
            pltpu.VMEM(home, f32),
            pltpu.VMEM((homes // 2, 2 * width, 2 * width), bf16),
            pltpu.VMEM((rows, width), bf16),
            pltpu.SemaphoreType.DMA((cell_count,)),
            pltpu.SemaphoreType.DMA((cell_count,)),
            pltpu.SemaphoreType.DMA((cell_count,)),
            pltpu.SemaphoreType.DMA((device_count,)),
            pltpu.SemaphoreType.DMA((device_count,)),
            pltpu.SemaphoreType.DMA((device_count,)),
            pltpu.SemaphoreType.DMA((device_count,)),
            pltpu.SemaphoreType.DMA((device_count,)),
            pltpu.SemaphoreType.DMA((device_count,)),
            pltpu.SemaphoreType.DMA((5,)),
        ],
        compiler_params=pltpu.CompilerParams(
            collective_id=0, has_side_effects=True, vmem_limit_bytes=60 * 1024 * 1024
        ),
    )(
        gains.reshape(blocks, near_count * width, width),
        near_blocks.reshape(-1),
        serve_block.reshape(row),
        serve_cell.reshape(row),
        serve_gain.reshape(row),
        power_init,
        avg_init.reshape(row),
    )
    return (average.reshape(rows), power)


def solution(mesh):
    return jax.shard_map(
        on_device,
        mesh=mesh,
        in_specs=(
            P("ue", "cell", None, None),
            P("ue", "cell"),
            P(("ue", "cell"), None),
            P(("ue", "cell")),
            P(("ue", "cell")),
            P(None, ("ue", "cell")),
            P(("ue", "cell")),
        ),
        out_specs=(P(("ue", "cell")), P(None, ("ue", "cell"))),
        check_vma=False,
    )
```

```python
import functools

import jax
import jax.numpy as jnp
from jax import lax
from jax.experimental import pallas as pl
from jax.experimental.pallas import tpu as pltpu
from jax.sharding import PartitionSpec as P

SLOTS = 4
NOISE_FLOOR = 0.5
KEEP_RATE = 0.7
NEW_RATE = 0.3
MESH = pl.DeviceIdType.MESH


def planner(
    ue_count, cell_count,
    gains_hbm, near, block_hbm, cell_hbm, gain_hbm, power_hbm, avg_hbm,
    avg_out, power_out,
    block_ref, cell_ref, gain_ref, gains, high, low, power, loads, tails, mine, parts_in, parts_out, terms_in, terms_out,
    levels, signal_power, log_rates, metrics, spread, pick_cell, put_cell,
    gains_sem, terms_send, terms_recv, sent, arrived, inputs_sem,
):
    device_count = ue_count * cell_count
    ue_at, cell_at = lax.axis_index("ue"), lax.axis_index("cell")
    me = ue_at * cell_count + cell_at
    home_blocks, subbands, width = levels.shape
    near_count = near.shape[0] // gains.shape[0]
    pairs = home_blocks // 2
    f32, bf16 = jnp.float32, jnp.bfloat16

    def device(number):
        return (number // cell_count, lax.rem(number, cell_count))

    inputs = [
        pltpu.make_async_copy(source, target, inputs_sem.at[place])
        for place, (source, target) in enumerate(
            [
                (power_hbm, mine), (cell_hbm, cell_ref), (block_hbm, block_ref),
                (gain_hbm, gain_ref), (avg_hbm, avg_out),
            ]
        )
    ]
    for copy in inputs:
        copy.start()
    barrier = pltpu.get_barrier_semaphore()

    def greet(step, carry):
        pl.semaphore_signal(
            barrier, inc=1, device_id=device(lax.rem(me + step, device_count)), device_id_type=MESH
        )
        return carry

    lax.fori_loop(1, device_count, greet, 0)

    def gains_copy(chunk):
        rows = pl.ds(chunk * home_blocks, home_blocks)
        return pltpu.make_async_copy(gains_hbm.at[rows], gains.at[rows], gains_sem.at[chunk])

    def terms_target(step):
        chips = cell_count // 2
        chip = lax.rem(cell_at // 2 + step // 2, chips)
        return chip * 2 + lax.rem(cell_at + step, 2)

    terms_order = list(range(2, cell_count)) + [1, 0]
    for step in terms_order:
        gains_copy(terms_target(step)).start()
    for copy in inputs:
        copy.wait()
    pl.semaphore_wait(barrier, device_count - 1)

    near_kind, far_kind, rest_kind, parts_kind = range(4)
    kind_counts = (
        ue_count - 1, device_count - ue_count, device_count - 1, device_count - 1
    )

    def spread_copy(table, kind, step):
        return pltpu.make_async_remote_copy(
            src_ref=table.at[me], dst_ref=table.at[me],
            send_sem=sent.at[kind], recv_sem=arrived.at[kind],
            device_id=device(lax.rem(me + step, device_count)), device_id_type=MESH,
        )

    def wait_all(semaphores, table, kind):
        rows = table.at[pl.ds(0, kind_counts[kind])]
        pltpu.make_async_copy(rows, rows, semaphores.at[kind]).wait()

    def send_loads():
        each_near(lambda step: spread_copy(loads, near_kind, step).start())
        each_far(lambda step: spread_copy(loads, far_kind, step).start())

    def send_tails():
        each_peer(lambda step: spread_copy(tails, rest_kind, step).start())

    def split_load(value):
        top = value.astype(bf16)
        loads[me] = top
        tails[me] = (value - top.astype(f32)).astype(bf16)

    def whole_load(block):
        return loads[block].astype(f32) + tails[block].astype(f32)

    def parts_copy(owner):
        step = lax.rem(owner - me + device_count, device_count)
        return pltpu.make_async_remote_copy(
            src_ref=parts_out.at[owner], dst_ref=parts_in.at[step],
            send_sem=sent.at[parts_kind], recv_sem=arrived.at[parts_kind],
            device_id=device(owner), device_id_type=MESH,
        )

    def terms_copy(step):
        target = terms_target(step)
        return pltpu.make_async_remote_copy(
            src_ref=terms_out.at[step], dst_ref=terms_in.at[step],
            send_sem=terms_send.at[step], recv_sem=terms_recv.at[step],
            device_id=(ue_at, target), device_id_type=MESH,
        )

    def each_peer(action):
        def body(step, carry):
            action(step)
            return carry

        lax.fori_loop(1, device_count, body, 0)

    def each_near(action):
        def body(step, carry):
            action(step * cell_count)
            return carry

        lax.fori_loop(1, ue_count, body, 0)

    def each_far(action):
        def body(step, carry):
            for other in range(1, cell_count):
                action(step * cell_count + other)
            return carry

        lax.fori_loop(0, ue_count, body, 0)

    def set_power(block, value):
        power[block] = value
        top = value.astype(bf16)
        high[block] = top
        low[block] = (value - top.astype(f32)).astype(bf16)

    def next_power(value, load):
        demand = 1.0 + load
        scale = (0.5 * subbands) / jnp.sum(demand, axis=0, keepdims=True)
        return 0.5 * value + demand * scale

    split_load(mine[...])
    send_loads()
    send_tails()
    spots = lax.broadcasted_iota(jnp.int32, (width, width), 0)
    for home in range(home_blocks):
        hot = (spots == cell_ref[home]).astype(f32)
        columns = slice((home % 2) * width, (home % 2 + 1) * width)
        pick_cell[home // 2, 0:width, columns] = hot.astype(bf16)
        pick_cell[home // 2, width : 2 * width, columns] = hot.astype(bf16)
        put_cell[home * width : (home + 1) * width, :] = hot.T.astype(bf16)
    wait_all(arrived, loads, near_kind)

    def start_high(index, carry):
        block = index * cell_count + cell_at
        high[block] = loads[block]
        return carry

    lax.fori_loop(0, ue_count, start_high, 0)

    def finish_loads():
        wait_all(arrived, loads, far_kind)
        wait_all(sent, loads, far_kind)
        wait_all(sent, loads, near_kind)

    def finish_power(turn):
        wait_all(arrived, tails, rest_kind)

        @pl.when(turn == 0)
        def _():
            def first(block, carry):
                set_power(block, whole_load(block))
                return carry

            lax.fori_loop(0, device_count, first, 0)

        @pl.when(turn > 0)
        def _():
            def later(block, carry):
                set_power(block, next_power(power[block], whole_load(block)))
                return carry

            lax.fori_loop(0, device_count, later, 0)

        set_power(me, mine[...])
        wait_all(sent, tails, rest_kind)

    def terms(target, step):
        def body(group, carry):
            for inner in range(8):
                home = group * 8 + inner
                block = target * home_blocks + home
                chosen = jnp.concatenate(
                    [high[near[block * near_count + k]] for k in range(near_count)], axis=1
                )
                total = jnp.dot(chosen, gains[block], preferred_element_type=f32)
                if step == 0:
                    levels[home] = total
                else:
                    terms_out[step, home] = total.astype(bf16)
            return carry

        lax.fori_loop(0, home_blocks // 8, body, 0)

    group_blocks = 16

    def gather(table, result):
        def body(pair, carry):
            names = jnp.concatenate([block_ref[2 * pair], block_ref[2 * pair + 1]], axis=1)
            total = jnp.zeros((subbands, 2 * width), f32)
            for first in range(0, device_count, group_blocks):
                left = table(first)
                found = jnp.dot(
                    left, pick_cell[pair, 0 : left.shape[1], :], preferred_element_type=f32
                )
                for inner in range(group_blocks):
                    total = jnp.where(
                        names == first + inner,
                        found[inner * subbands : (inner + 1) * subbands],
                        total,
                    )
            result[2 * pair] = total[:, :width]
            result[2 * pair + 1] = total[:, width:]
            return carry

        lax.fori_loop(0, pairs, body, 0)

    def power_rows(first):
        rows = slice(first, first + group_blocks)
        both = jnp.concatenate([high[rows], low[rows]], axis=2)
        return both.reshape(group_blocks * subbands, 2 * width)

    def load_rows(first):
        return loads[first : first + group_blocks].reshape(group_blocks * subbands, width)

    def finish_average():
        gather(load_rows, spread)
        for home in range(home_blocks):
            share = metrics[home] / spread[home]
            gained = jnp.sum(share * log_rates[home], axis=0, keepdims=True)
            avg_out[home] = KEEP_RATE * avg_out[home] + NEW_RATE * gained

    piece = 8

    def slot(turn, carry):
        for step in terms_order:
            target = terms_target(step)

            @pl.when(turn == 0)
            def _():
                gains_copy(target).wait()

            terms(target, step)
            if step > 0:
                terms_copy(step).start()

        finish_loads()

        @pl.when(turn > 0)
        def _():
            finish_average()

        finish_power(turn)
        gather(power_rows, signal_power)
        for step in range(1, cell_count):
            terms_copy(step).wait_recv()
        for home in range(home_blocks):
            level = levels[home]
            for step in range(1, cell_count):
                level = level + terms_in[step, home].astype(f32)
            signal = gain_ref[home] * signal_power[home]
            rate = jnp.log1p(signal / (level + NOISE_FLOOR))
            log_rates[home] = rate
            metrics[home] = rate / avg_out[home]
        names = jnp.concatenate([block_ref[home] for home in range(home_blocks)], axis=1)

        def scatter(index, inner_carry):
            first = lax.rem(me // piece + 1 + index, device_count // piece) * piece
            metric = jnp.concatenate([metrics[home] for home in range(home_blocks)], axis=1)
            left = jnp.concatenate(
                [
                    jnp.where(names == first + inner, metric, 0.0).astype(bf16)
                    for inner in range(piece)
                ],
                axis=0,
            )
            summed = jnp.dot(left, put_cell[...], preferred_element_type=f32)
            for inner in range(piece):
                owner = first + inner
                parts_out[owner] = summed[inner * subbands : (inner + 1) * subbands].astype(bf16)

                @pl.when(owner != me)
                def _():
                    parts_copy(owner).start()

            return inner_carry

        lax.fori_loop(0, device_count // piece, scatter, 0)
        for step in range(1, cell_count):
            terms_copy(step).wait_send()

        wait_all(arrived, parts_in, parts_kind)
        load = parts_out[me].astype(f32)
        for step in range(1, device_count):
            load = load + parts_in[step].astype(f32)
        split_load(load)
        send_loads()

        @pl.when(turn < SLOTS - 1)
        def _():
            send_tails()

        mine[...] = next_power(mine[...], load)
        wait_all(arrived, loads, near_kind)

        @pl.when(turn < SLOTS - 1)
        def _():
            def update(index, inner_carry):
                block = index * cell_count + cell_at
                high[block] = next_power(power[block], loads[block].astype(f32)).astype(bf16)
                return inner_carry

            lax.fori_loop(0, ue_count, update, 0)
            high[me] = mine[...].astype(bf16)

        wait_all(sent, parts_out, parts_kind)
        return carry

    lax.fori_loop(0, SLOTS, slot, 0)
    finish_loads()
    finish_average()
    power_out[...] = mine[...]


def on_device(gains, near_blocks, serve_block, serve_cell, serve_gain, power_init, avg_init):
    ue_count = lax.axis_size("ue")
    cell_count = lax.axis_size("cell")
    device_count = ue_count * cell_count
    blocks, near_count, width, _ = gains.shape
    rows = serve_gain.shape[0]
    homes = rows // width
    subbands = power_init.shape[0]
    f32, bf16 = jnp.float32, jnp.bfloat16
    in_vmem = pl.BlockSpec(memory_space=pltpu.VMEM)
    table = (device_count, subbands, width)
    home = (homes, subbands, width)
    row = (homes, 1, width)
    average, power = pl.pallas_call(
        functools.partial(planner, ue_count, cell_count),
        out_shape=(
            jax.ShapeDtypeStruct(row, f32),
            jax.ShapeDtypeStruct(power_init.shape, f32),
        ),
        in_specs=[
            pl.BlockSpec(memory_space=pl.ANY),
            pl.BlockSpec(memory_space=pltpu.SMEM),
        ]
        + [pl.BlockSpec(memory_space=pl.ANY)] * 5,
        out_specs=(in_vmem, in_vmem),
        scratch_shapes=[
            pltpu.VMEM(row, jnp.int32),
            pltpu.VMEM(row, jnp.int32),
            pltpu.VMEM(row, f32),
            pltpu.VMEM((blocks, near_count * width, width), bf16),
            pltpu.VMEM(table, bf16),
            pltpu.VMEM(table, bf16),
            pltpu.VMEM(table, f32),
            pltpu.VMEM(table, bf16),
            pltpu.VMEM(table, bf16),
            pltpu.VMEM((subbands, width), f32),
            pltpu.VMEM(table, bf16),
            pltpu.VMEM(table, bf16),
            pltpu.VMEM((cell_count,) + home, bf16),
            pltpu.VMEM((cell_count,) + home, bf16),
            pltpu.VMEM(home, f32),
            pltpu.VMEM(home, f32),
            pltpu.VMEM(home, f32),
            pltpu.VMEM(home, f32),
            pltpu.VMEM(home, f32),
            pltpu.VMEM((homes // 2, 2 * width, 2 * width), bf16),
            pltpu.VMEM((rows, width), bf16),
            pltpu.SemaphoreType.DMA((cell_count,)),
            pltpu.SemaphoreType.DMA((cell_count,)),
            pltpu.SemaphoreType.DMA((cell_count,)),
            pltpu.SemaphoreType.DMA((4,)),
            pltpu.SemaphoreType.DMA((4,)),
            pltpu.SemaphoreType.DMA((5,)),
        ],
        compiler_params=pltpu.CompilerParams(
            collective_id=0, has_side_effects=True, vmem_limit_bytes=60 * 1024 * 1024
        ),
    )(
        gains.reshape(blocks, near_count * width, width),
        near_blocks.reshape(-1),
        serve_block.reshape(row),
        serve_cell.reshape(row),
        serve_gain.reshape(row),
        power_init,
        avg_init.reshape(row),
    )
    return (average.reshape(rows), power)


def solution(mesh):
    return jax.shard_map(
        on_device,
        mesh=mesh,
        in_specs=(
            P("ue", "cell", None, None),
            P("ue", "cell"),
            P(("ue", "cell"), None),
            P(("ue", "cell")),
            P(("ue", "cell")),
            P(None, ("ue", "cell")),
            P(("ue", "cell")),
        ),
        out_specs=(P(("ue", "cell")), P(None, ("ue", "cell"))),
        check_vma=False,
    )
```

```python
import functools

import jax
import jax.numpy as jnp
from jax import lax
from jax.experimental import pallas as pl
from jax.experimental.pallas import tpu as pltpu
from jax.sharding import PartitionSpec as P

SLOTS = 4
NOISE_FLOOR = 0.5
KEEP_RATE = 0.7
NEW_RATE = 0.3
MESH = pl.DeviceIdType.MESH


def planner(
    ue_count, cell_count,
    gains_hbm, near, block_hbm, cell_hbm, gain_hbm, power_hbm, avg_hbm,
    avg_out, power_out,
    block_ref, cell_ref, gain_ref, gains, high, low, power, loads, tails, mine, parts_in, parts_out, terms_in, terms_out,
    levels, signal_power, log_rates, metrics, spread, pick_cell, put_cell,
    gains_sem, terms_send, terms_recv, sent, arrived, inputs_sem,
):
    device_count = ue_count * cell_count
    ue_at, cell_at = lax.axis_index("ue"), lax.axis_index("cell")
    me = ue_at * cell_count + cell_at
    home_blocks, subbands, width = levels.shape
    near_count = near.shape[0] // gains.shape[0]
    pairs = home_blocks // 2
    f32, bf16 = jnp.float32, jnp.bfloat16

    def device(number):
        return (number // cell_count, lax.rem(number, cell_count))

    inputs = [
        pltpu.make_async_copy(source, target, inputs_sem.at[place])
        for place, (source, target) in enumerate(
            [
                (power_hbm, mine), (cell_hbm, cell_ref), (block_hbm, block_ref),
                (gain_hbm, gain_ref), (avg_hbm, avg_out),
            ]
        )
    ]
    for copy in inputs:
        copy.start()
    barrier = pltpu.get_barrier_semaphore()

    def greet(step, carry):
        pl.semaphore_signal(
            barrier, inc=1, device_id=device(lax.rem(me + step, device_count)), device_id_type=MESH
        )
        return carry

    lax.fori_loop(1, device_count, greet, 0)

    def gains_copy(chunk):
        rows = pl.ds(chunk * home_blocks, home_blocks)
        return pltpu.make_async_copy(gains_hbm.at[rows], gains.at[rows], gains_sem.at[chunk])

    def terms_target(step):
        chips = cell_count // 2
        chip = lax.rem(cell_at // 2 + step // 2, chips)
        return chip * 2 + lax.rem(cell_at + step, 2)

    terms_order = list(range(2, cell_count)) + [1, 0]
    for step in terms_order:
        gains_copy(terms_target(step)).start()
    for copy in inputs:
        copy.wait()
    pl.semaphore_wait(barrier, device_count - 1)

    near_kind, far_kind, rest_kind, parts_kind = range(4)
    kind_counts = (
        ue_count - 1, device_count - ue_count, device_count - 1, device_count - 1
    )

    def spread_copy(table, kind, step):
        return pltpu.make_async_remote_copy(
            src_ref=table.at[me], dst_ref=table.at[me],
            send_sem=sent.at[kind], recv_sem=arrived.at[kind],
            device_id=device(lax.rem(me + step, device_count)), device_id_type=MESH,
        )

    def wait_all(semaphores, table, kind):
        rows = table.at[pl.ds(0, kind_counts[kind])]
        pltpu.make_async_copy(rows, rows, semaphores.at[kind]).wait()

    def send_loads():
        each_near(lambda step: spread_copy(loads, near_kind, step).start())
        each_far(lambda step: spread_copy(loads, far_kind, step).start())

    def send_tails():
        each_peer(lambda step: spread_copy(tails, rest_kind, step).start())

    def split_load(value):
        top = value.astype(bf16)
        loads[me] = top
        tails[me] = (value - top.astype(f32)).astype(bf16)

    def whole_load(block):
        return loads[block].astype(f32) + tails[block].astype(f32)

    def parts_copy(owner):
        step = lax.rem(owner - me + device_count, device_count)
        return pltpu.make_async_remote_copy(
            src_ref=parts_out.at[owner], dst_ref=parts_in.at[step],
            send_sem=sent.at[parts_kind], recv_sem=arrived.at[parts_kind],
            device_id=device(owner), device_id_type=MESH,
        )

    def terms_copy(step):
        target = terms_target(step)
        return pltpu.make_async_remote_copy(
            src_ref=terms_out.at[step], dst_ref=terms_in.at[step],
            send_sem=terms_send.at[step], recv_sem=terms_recv.at[step],
            device_id=(ue_at, target), device_id_type=MESH,
        )

    def each_peer(action):
        def body(step, carry):
            action(step)
            return carry

        lax.fori_loop(1, device_count, body, 0)

    def each_near(action):
        def body(step, carry):
            action(step * cell_count)
            return carry

        lax.fori_loop(1, ue_count, body, 0)

    def each_far(action):
        def body(step, carry):
            for other in range(1, cell_count):
                action(step * cell_count + other)
            return carry

        lax.fori_loop(0, ue_count, body, 0)

    def each_block(count, action):
        def body(group, carry):
            for inner in range(4):
                action(group * 4 + inner)
            return carry

        lax.fori_loop(0, count // 4, body, 0)

    def set_power(block, value):
        power[block] = value
        top = value.astype(bf16)
        high[block] = top
        low[block] = (value - top.astype(f32)).astype(bf16)

    def next_power(value, load):
        demand = 1.0 + load
        scale = (0.5 * subbands) / jnp.sum(demand, axis=0, keepdims=True)
        return 0.5 * value + demand * scale

    split_load(mine[...])
    send_loads()
    send_tails()
    spots = lax.broadcasted_iota(jnp.int32, (width, width), 0)
    for home in range(home_blocks):
        hot = (spots == cell_ref[home]).astype(f32)
        columns = slice((home % 2) * width, (home % 2 + 1) * width)
        pick_cell[home // 2, 0:width, columns] = hot.astype(bf16)
        pick_cell[home // 2, width : 2 * width, columns] = hot.astype(bf16)
        put_cell[home * width : (home + 1) * width, :] = hot.T.astype(bf16)
    wait_all(arrived, loads, near_kind)

    def start_high(index, carry):
        block = index * cell_count + cell_at
        high[block] = loads[block]
        return carry

    lax.fori_loop(0, ue_count, start_high, 0)

    def finish_loads():
        wait_all(arrived, loads, far_kind)
        wait_all(sent, loads, far_kind)
        wait_all(sent, loads, near_kind)

    def finish_power(turn):
        wait_all(arrived, tails, rest_kind)

        @pl.when(turn == 0)
        def _():
            each_block(device_count, lambda block: set_power(block, whole_load(block)))

        @pl.when(turn > 0)
        def _():
            def later(block):
                set_power(block, next_power(power[block], whole_load(block)))

            each_block(device_count, later)

        set_power(me, mine[...])
        wait_all(sent, tails, rest_kind)

    def terms(target, step):
        def body(group, carry):
            for inner in range(16):
                home = group * 16 + inner
                block = target * home_blocks + home
                chosen = jnp.concatenate(
                    [high[near[block * near_count + k]] for k in range(near_count)], axis=1
                )
                total = jnp.dot(chosen, gains[block], preferred_element_type=f32)
                if step == 0:
                    levels[home] = total
                else:
                    terms_out[step, home] = total.astype(bf16)
            return carry

        lax.fori_loop(0, home_blocks // 16, body, 0)

    group_blocks = 16

    def gather(table, result):
        def one(pair):
            names = jnp.concatenate([block_ref[2 * pair], block_ref[2 * pair + 1]], axis=1)
            total = jnp.zeros((subbands, 2 * width), f32)
            for first in range(0, device_count, group_blocks):
                left = table(first)
                found = jnp.dot(
                    left, pick_cell[pair, 0 : left.shape[1], :], preferred_element_type=f32
                )
                for inner in range(group_blocks):
                    total = jnp.where(
                        names == first + inner,
                        found[inner * subbands : (inner + 1) * subbands],
                        total,
                    )
            result[2 * pair] = total[:, :width]
            result[2 * pair + 1] = total[:, width:]

        each_block(pairs, one)

    def power_rows(first):
        rows = slice(first, first + group_blocks)
        both = jnp.concatenate([high[rows], low[rows]], axis=2)
        return both.reshape(group_blocks * subbands, 2 * width)

    def load_rows(first):
        return loads[first : first + group_blocks].reshape(group_blocks * subbands, width)

    def finish_average():
        gather(load_rows, spread)
        for home in range(home_blocks):
            share = metrics[home] / spread[home]
            gained = jnp.sum(share * log_rates[home], axis=0, keepdims=True)
            avg_out[home] = KEEP_RATE * avg_out[home] + NEW_RATE * gained

    piece = 8

    def slot(turn, carry):
        for step in terms_order:
            target = terms_target(step)

            @pl.when(turn == 0)
            def _():
                gains_copy(target).wait()

            terms(target, step)
            if step > 0:
                terms_copy(step).start()

        finish_loads()

        @pl.when(turn > 0)
        def _():
            finish_average()

        finish_power(turn)
        gather(power_rows, signal_power)
        for step in range(1, cell_count):
            terms_copy(step).wait_recv()
        for home in range(home_blocks):
            level = levels[home]
            for step in range(1, cell_count):
                level = level + terms_in[step, home].astype(f32)
            signal = gain_ref[home] * signal_power[home]
            rate = jnp.log1p(signal / (level + NOISE_FLOOR))
            log_rates[home] = rate
            metrics[home] = rate / avg_out[home]
        names = jnp.concatenate([block_ref[home] for home in range(home_blocks)], axis=1)

        def scatter(index, inner_carry):
            first = lax.rem(me // piece + 1 + index, device_count // piece) * piece
            metric = jnp.concatenate([metrics[home] for home in range(home_blocks)], axis=1)
            left = jnp.concatenate(
                [
                    jnp.where(names == first + inner, metric, 0.0).astype(bf16)
                    for inner in range(piece)
                ],
                axis=0,
            )
            summed = jnp.dot(left, put_cell[...], preferred_element_type=f32)
            for inner in range(piece):
                owner = first + inner
                parts_out[owner] = summed[inner * subbands : (inner + 1) * subbands].astype(bf16)

                @pl.when(owner != me)
                def _():
                    parts_copy(owner).start()

            return inner_carry

        lax.fori_loop(0, device_count // piece, scatter, 0)
        for step in range(1, cell_count):
            terms_copy(step).wait_send()

        wait_all(arrived, parts_in, parts_kind)
        load = parts_out[me].astype(f32)
        for step in range(1, device_count):
            load = load + parts_in[step].astype(f32)
        split_load(load)
        send_loads()

        @pl.when(turn < SLOTS - 1)
        def _():
            send_tails()

        mine[...] = next_power(mine[...], load)
        wait_all(arrived, loads, near_kind)

        @pl.when(turn < SLOTS - 1)
        def _():
            def update(index):
                block = index * cell_count + cell_at
                high[block] = next_power(power[block], loads[block].astype(f32)).astype(bf16)

            each_block(ue_count, update)
            high[me] = mine[...].astype(bf16)

        wait_all(sent, parts_out, parts_kind)
        return carry

    lax.fori_loop(0, SLOTS, slot, 0)
    finish_loads()
    finish_average()
    power_out[...] = mine[...]


def on_device(gains, near_blocks, serve_block, serve_cell, serve_gain, power_init, avg_init):
    ue_count = lax.axis_size("ue")
    cell_count = lax.axis_size("cell")
    device_count = ue_count * cell_count
    blocks, near_count, width, _ = gains.shape
    rows = serve_gain.shape[0]
    homes = rows // width
    subbands = power_init.shape[0]
    f32, bf16 = jnp.float32, jnp.bfloat16
    in_vmem = pl.BlockSpec(memory_space=pltpu.VMEM)
    table = (device_count, subbands, width)
    home = (homes, subbands, width)
    row = (homes, 1, width)
    average, power = pl.pallas_call(
        functools.partial(planner, ue_count, cell_count),
        out_shape=(
            jax.ShapeDtypeStruct(row, f32),
            jax.ShapeDtypeStruct(power_init.shape, f32),
        ),
        in_specs=[
            pl.BlockSpec(memory_space=pl.ANY),
            pl.BlockSpec(memory_space=pltpu.SMEM),
        ]
        + [pl.BlockSpec(memory_space=pl.ANY)] * 5,
        out_specs=(in_vmem, in_vmem),
        scratch_shapes=[
            pltpu.VMEM(row, jnp.int32),
            pltpu.VMEM(row, jnp.int32),
            pltpu.VMEM(row, f32),
            pltpu.VMEM((blocks, near_count * width, width), bf16),
            pltpu.VMEM(table, bf16),
            pltpu.VMEM(table, bf16),
            pltpu.VMEM(table, f32),
            pltpu.VMEM(table, bf16),
            pltpu.VMEM(table, bf16),
            pltpu.VMEM((subbands, width), f32),
            pltpu.VMEM(table, bf16),
            pltpu.VMEM(table, bf16),
            pltpu.VMEM((cell_count,) + home, bf16),
            pltpu.VMEM((cell_count,) + home, bf16),
            pltpu.VMEM(home, f32),
            pltpu.VMEM(home, f32),
            pltpu.VMEM(home, f32),
            pltpu.VMEM(home, f32),
            pltpu.VMEM(home, f32),
            pltpu.VMEM((homes // 2, 2 * width, 2 * width), bf16),
            pltpu.VMEM((rows, width), bf16),
            pltpu.SemaphoreType.DMA((cell_count,)),
            pltpu.SemaphoreType.DMA((cell_count,)),
            pltpu.SemaphoreType.DMA((cell_count,)),
            pltpu.SemaphoreType.DMA((4,)),
            pltpu.SemaphoreType.DMA((4,)),
            pltpu.SemaphoreType.DMA((5,)),
        ],
        compiler_params=pltpu.CompilerParams(
            collective_id=0, has_side_effects=True, vmem_limit_bytes=60 * 1024 * 1024
        ),
    )(
        gains.reshape(blocks, near_count * width, width),
        near_blocks.reshape(-1),
        serve_block.reshape(row),
        serve_cell.reshape(row),
        serve_gain.reshape(row),
        power_init,
        avg_init.reshape(row),
    )
    return (average.reshape(rows), power)


def solution(mesh):
    return jax.shard_map(
        on_device,
        mesh=mesh,
        in_specs=(
            P("ue", "cell", None, None),
            P("ue", "cell"),
            P(("ue", "cell"), None),
            P(("ue", "cell")),
            P(("ue", "cell")),
            P(None, ("ue", "cell")),
            P(("ue", "cell")),
        ),
        out_specs=(P(("ue", "cell")), P(None, ("ue", "cell"))),
        check_vma=False,
    )
```

```python
import functools

import jax
import jax.numpy as jnp
from jax import lax
from jax.experimental import pallas as pl
from jax.experimental.pallas import tpu as pltpu
from jax.sharding import PartitionSpec as P

SLOTS = 4
NOISE_FLOOR = 0.5
KEEP_RATE = 0.7
NEW_RATE = 0.3
MESH = pl.DeviceIdType.MESH


def planner(
    ue_count, cell_count,
    gains_hbm, near, block_hbm, cell_hbm, gain_hbm, power_hbm, avg_hbm,
    avg_out, power_out,
    block_ref, cell_ref, gain_ref, gains, high, low, power, loads, tails, mine, parts_in, parts_out, terms_in, terms_out,
    levels, signal_power, log_rates, metrics, spread, pick_cell, put_cell,
    gains_sem, terms_send, terms_recv, sent, arrived, inputs_sem,
):
    device_count = ue_count * cell_count
    ue_at, cell_at = lax.axis_index("ue"), lax.axis_index("cell")
    me = ue_at * cell_count + cell_at
    home_blocks, subbands, width = levels.shape
    near_count = near.shape[0] // gains.shape[0]
    pairs = home_blocks // 2
    f32, bf16 = jnp.float32, jnp.bfloat16

    def device(number):
        return (number // cell_count, lax.rem(number, cell_count))

    inputs = [
        pltpu.make_async_copy(source, target, inputs_sem.at[place])
        for place, (source, target) in enumerate(
            [
                (power_hbm, mine), (cell_hbm, cell_ref), (block_hbm, block_ref),
                (gain_hbm, gain_ref), (avg_hbm, avg_out),
            ]
        )
    ]
    for copy in inputs:
        copy.start()
    barrier = pltpu.get_barrier_semaphore()

    def greet(step, carry):
        pl.semaphore_signal(
            barrier, inc=1, device_id=device(lax.rem(me + step, device_count)), device_id_type=MESH
        )
        return carry

    lax.fori_loop(1, device_count, greet, 0)

    def gains_copy(chunk):
        rows = pl.ds(chunk * home_blocks, home_blocks)
        return pltpu.make_async_copy(gains_hbm.at[rows], gains.at[rows], gains_sem.at[chunk])

    def terms_target(step):
        chips = cell_count // 2
        chip = lax.rem(cell_at // 2 + step // 2, chips)
        return chip * 2 + lax.rem(cell_at + step, 2)

    terms_order = list(range(2, cell_count)) + [1, 0]
    for step in terms_order:
        gains_copy(terms_target(step)).start()
    for copy in inputs:
        copy.wait()
    pl.semaphore_wait(barrier, device_count - 1)

    near_kind, far_kind, rest_kind, parts_kind = range(4)
    kind_counts = (
        ue_count - 1, device_count - ue_count, device_count - 1, device_count - 1
    )

    def spread_copy(table, kind, step):
        return pltpu.make_async_remote_copy(
            src_ref=table.at[me], dst_ref=table.at[me],
            send_sem=sent.at[kind], recv_sem=arrived.at[kind],
            device_id=device(lax.rem(me + step, device_count)), device_id_type=MESH,
        )

    def wait_all(semaphores, table, kind):
        rows = table.at[pl.ds(0, kind_counts[kind])]
        pltpu.make_async_copy(rows, rows, semaphores.at[kind]).wait()

    def send_loads():
        each_near(lambda step: spread_copy(loads, near_kind, step).start())
        each_far(lambda step: spread_copy(loads, far_kind, step).start())

    def send_tails():
        each_peer(lambda step: spread_copy(tails, rest_kind, step).start())

    def split_load(value):
        top = value.astype(bf16)
        loads[me] = top
        tails[me] = (value - top.astype(f32)).astype(bf16)

    def whole_load(block):
        return loads[block].astype(f32) + tails[block].astype(f32)

    def parts_copy(owner):
        step = lax.rem(owner - me + device_count, device_count)
        return pltpu.make_async_remote_copy(
            src_ref=parts_out.at[owner], dst_ref=parts_in.at[step],
            send_sem=sent.at[parts_kind], recv_sem=arrived.at[parts_kind],
            device_id=device(owner), device_id_type=MESH,
        )

    def terms_copy(step):
        target = terms_target(step)
        return pltpu.make_async_remote_copy(
            src_ref=terms_out.at[step], dst_ref=terms_in.at[step],
            send_sem=terms_send.at[step], recv_sem=terms_recv.at[step],
            device_id=(ue_at, target), device_id_type=MESH,
        )

    def each_peer(action):
        def body(step, carry):
            action(step)
            return carry

        lax.fori_loop(1, device_count, body, 0)

    def each_near(action):
        for step in range(1, ue_count):
            action(step * cell_count)

    def each_far(action):
        def body(step, carry):
            for other in range(1, cell_count):
                action(step * cell_count + other)
            return carry

        lax.fori_loop(0, ue_count, body, 0)

    def each_block(count, action):
        def body(group, carry):
            for inner in range(4):
                action(group * 4 + inner)
            return carry

        lax.fori_loop(0, count // 4, body, 0)

    def set_power(block, value):
        power[block] = value
        top = value.astype(bf16)
        high[block] = top
        low[block] = (value - top.astype(f32)).astype(bf16)

    def next_power(value, load):
        demand = 1.0 + load
        scale = (0.5 * subbands) / jnp.sum(demand, axis=0, keepdims=True)
        return 0.5 * value + demand * scale

    split_load(mine[...])
    send_loads()
    send_tails()
    spots = lax.broadcasted_iota(jnp.int32, (width, width), 0)
    for home in range(home_blocks):
        hot = (spots == cell_ref[home]).astype(f32)
        columns = slice((home % 2) * width, (home % 2 + 1) * width)
        pick_cell[home // 2, 0:width, columns] = hot.astype(bf16)
        pick_cell[home // 2, width : 2 * width, columns] = hot.astype(bf16)
        put_cell[home * width : (home + 1) * width, :] = hot.T.astype(bf16)
    wait_all(arrived, loads, near_kind)

    def start_high(index, carry):
        block = index * cell_count + cell_at
        high[block] = loads[block]
        return carry

    lax.fori_loop(0, ue_count, start_high, 0)

    def finish_loads():
        wait_all(arrived, loads, far_kind)
        wait_all(sent, loads, far_kind)
        wait_all(sent, loads, near_kind)

    def finish_power(turn):
        wait_all(arrived, tails, rest_kind)

        @pl.when(turn == 0)
        def _():
            each_block(device_count, lambda block: set_power(block, whole_load(block)))

        @pl.when(turn > 0)
        def _():
            def later(block):
                set_power(block, next_power(power[block], whole_load(block)))

            each_block(device_count, later)

        set_power(me, mine[...])
        wait_all(sent, tails, rest_kind)

    def terms(target, step):
        def body(group, carry):
            for inner in range(16):
                home = group * 16 + inner
                block = target * home_blocks + home
                chosen = jnp.concatenate(
                    [high[near[block * near_count + k]] for k in range(near_count)], axis=1
                )
                total = jnp.dot(chosen, gains[block], preferred_element_type=f32)
                if step == 0:
                    levels[home] = total
                else:
                    terms_out[step, home] = total.astype(bf16)
            return carry

        lax.fori_loop(0, home_blocks // 16, body, 0)

    group_blocks = 16

    def gather(table, result):
        def one(pair):
            names = jnp.concatenate([block_ref[2 * pair], block_ref[2 * pair + 1]], axis=1)
            total = jnp.zeros((subbands, 2 * width), f32)
            for first in range(0, device_count, group_blocks):
                left = table(first)
                found = jnp.dot(
                    left, pick_cell[pair, 0 : left.shape[1], :], preferred_element_type=f32
                )
                for inner in range(group_blocks):
                    total = jnp.where(
                        names == first + inner,
                        found[inner * subbands : (inner + 1) * subbands],
                        total,
                    )
            result[2 * pair] = total[:, :width]
            result[2 * pair + 1] = total[:, width:]

        each_block(pairs, one)

    def power_rows(first):
        rows = slice(first, first + group_blocks)
        both = jnp.concatenate([high[rows], low[rows]], axis=2)
        return both.reshape(group_blocks * subbands, 2 * width)

    def load_rows(first):
        return loads[first : first + group_blocks].reshape(group_blocks * subbands, width)

    def finish_average():
        gather(load_rows, spread)
        for home in range(home_blocks):
            share = metrics[home] / spread[home]
            gained = jnp.sum(share * log_rates[home], axis=0, keepdims=True)
            avg_out[home] = KEEP_RATE * avg_out[home] + NEW_RATE * gained

    piece = 8

    def slot(turn, carry):
        for step in terms_order:
            target = terms_target(step)

            @pl.when(turn == 0)
            def _():
                gains_copy(target).wait()

            terms(target, step)
            if step > 0:
                terms_copy(step).start()

        finish_loads()

        @pl.when(turn > 0)
        def _():
            finish_average()

        finish_power(turn)
        gather(power_rows, signal_power)
        for step in range(1, cell_count):
            terms_copy(step).wait_recv()
        for home in range(home_blocks):
            level = levels[home]
            for step in range(1, cell_count):
                level = level + terms_in[step, home].astype(f32)
            signal = gain_ref[home] * signal_power[home]
            rate = jnp.log1p(signal / (level + NOISE_FLOOR))
            log_rates[home] = rate
            metrics[home] = rate / avg_out[home]
        names = jnp.concatenate([block_ref[home] for home in range(home_blocks)], axis=1)

        def scatter(index, inner_carry):
            first = lax.rem(me // piece + 1 + index, device_count // piece) * piece
            metric = jnp.concatenate([metrics[home] for home in range(home_blocks)], axis=1)
            left = jnp.concatenate(
                [
                    jnp.where(names == first + inner, metric, 0.0).astype(bf16)
                    for inner in range(piece)
                ],
                axis=0,
            )
            summed = jnp.dot(left, put_cell[...], preferred_element_type=f32)
            for inner in range(piece):
                owner = first + inner
                parts_out[owner] = summed[inner * subbands : (inner + 1) * subbands].astype(bf16)

                @pl.when(owner != me)
                def _():
                    parts_copy(owner).start()

            return inner_carry

        def scatter_two(group, inner_carry):
            return scatter(2 * group + 1, scatter(2 * group, inner_carry))

        lax.fori_loop(0, device_count // piece // 2, scatter_two, 0)
        for step in range(1, cell_count):
            terms_copy(step).wait_send()

        wait_all(arrived, parts_in, parts_kind)
        load = parts_out[me].astype(f32)
        for step in range(1, device_count):
            load = load + parts_in[step].astype(f32)
        split_load(load)
        send_loads()

        @pl.when(turn < SLOTS - 1)
        def _():
            send_tails()

        mine[...] = next_power(mine[...], load)
        wait_all(arrived, loads, near_kind)

        @pl.when(turn < SLOTS - 1)
        def _():
            def update(index):
                block = index * cell_count + cell_at
                high[block] = next_power(power[block], loads[block].astype(f32)).astype(bf16)

            each_block(ue_count, update)
            high[me] = mine[...].astype(bf16)

        wait_all(sent, parts_out, parts_kind)
        return carry

    lax.fori_loop(0, SLOTS, slot, 0)
    finish_loads()
    finish_average()
    power_out[...] = mine[...]


def on_device(gains, near_blocks, serve_block, serve_cell, serve_gain, power_init, avg_init):
    ue_count = lax.axis_size("ue")
    cell_count = lax.axis_size("cell")
    device_count = ue_count * cell_count
    blocks, near_count, width, _ = gains.shape
    rows = serve_gain.shape[0]
    homes = rows // width
    subbands = power_init.shape[0]
    f32, bf16 = jnp.float32, jnp.bfloat16
    in_vmem = pl.BlockSpec(memory_space=pltpu.VMEM)
    table = (device_count, subbands, width)
    home = (homes, subbands, width)
    row = (homes, 1, width)
    average, power = pl.pallas_call(
        functools.partial(planner, ue_count, cell_count),
        out_shape=(
            jax.ShapeDtypeStruct(row, f32),
            jax.ShapeDtypeStruct(power_init.shape, f32),
        ),
        in_specs=[
            pl.BlockSpec(memory_space=pl.ANY),
            pl.BlockSpec(memory_space=pltpu.SMEM),
        ]
        + [pl.BlockSpec(memory_space=pl.ANY)] * 5,
        out_specs=(in_vmem, in_vmem),
        scratch_shapes=[
            pltpu.VMEM(row, jnp.int32),
            pltpu.VMEM(row, jnp.int32),
            pltpu.VMEM(row, f32),
            pltpu.VMEM((blocks, near_count * width, width), bf16),
            pltpu.VMEM(table, bf16),
            pltpu.VMEM(table, bf16),
            pltpu.VMEM(table, f32),
            pltpu.VMEM(table, bf16),
            pltpu.VMEM(table, bf16),
            pltpu.VMEM((subbands, width), f32),
            pltpu.VMEM(table, bf16),
            pltpu.VMEM(table, bf16),
            pltpu.VMEM((cell_count,) + home, bf16),
            pltpu.VMEM((cell_count,) + home, bf16),
            pltpu.VMEM(home, f32),
            pltpu.VMEM(home, f32),
            pltpu.VMEM(home, f32),
            pltpu.VMEM(home, f32),
            pltpu.VMEM(home, f32),
            pltpu.VMEM((homes // 2, 2 * width, 2 * width), bf16),
            pltpu.VMEM((rows, width), bf16),
            pltpu.SemaphoreType.DMA((cell_count,)),
            pltpu.SemaphoreType.DMA((cell_count,)),
            pltpu.SemaphoreType.DMA((cell_count,)),
            pltpu.SemaphoreType.DMA((4,)),
            pltpu.SemaphoreType.DMA((4,)),
            pltpu.SemaphoreType.DMA((5,)),
        ],
        compiler_params=pltpu.CompilerParams(
            collective_id=0, has_side_effects=True, vmem_limit_bytes=60 * 1024 * 1024
        ),
    )(
        gains.reshape(blocks, near_count * width, width),
        near_blocks.reshape(-1),
        serve_block.reshape(row),
        serve_cell.reshape(row),
        serve_gain.reshape(row),
        power_init,
        avg_init.reshape(row),
    )
    return (average.reshape(rows), power)


def solution(mesh):
    return jax.shard_map(
        on_device,
        mesh=mesh,
        in_specs=(
            P("ue", "cell", None, None),
            P("ue", "cell"),
            P(("ue", "cell"), None),
            P(("ue", "cell")),
            P(("ue", "cell")),
            P(None, ("ue", "cell")),
            P(("ue", "cell")),
        ),
        out_specs=(P(("ue", "cell")), P(None, ("ue", "cell"))),
        check_vma=False,
    )
```
